256 devices in a mesh: tile: 64 (over x, z, core), pos: 4 (over y).
Axes of the slice: x: 4, y: 4, z: 8, core: 2. Of those that a mesh axis runs over, the one named last changes fastest.
Arguments:
- obj_real: float32 [4, 16384, 256], P(None, ('tile', 'pos')), may hold values from 0.5 to 1.5
- obj_imag: float32 [4, 16384, 256], P(None, ('tile', 'pos')), may hold values from -4 to 4
- probe: float32 [2, 128, 128], replicated, may hold values from -6 to 6
- fresnel_phase: float32 [33], replicated, may hold values from -3.140625 to 3.140625
- row_offset: int32 [4096], P('tile'), may hold values from 0 to 255
- col_offset: int32 [4096], P('tile'), may hold values from 0 to 128
- live_count: int32 [64], P('tile'), may hold values from 16 to 64, as said below
- measured: bfloat16 [4096, 128, 128], P('tile'), may hold values from 0.19921875 to 2
Outputs:
- grad_real: float32 [4, 16384, 256], P(None, ('tile', 'pos'))
- grad_imag: float32 [4, 16384, 256], P(None, ('tile', 'pos'))
The draws below stay inside these ranges and needn't reach their ends.
Inputs may be any that keep to these rules, and one draw needn't show every extreme that they name: `row_offset`: row offsets count from the first of the 256 rows of the position's band. Band g uses its first live_count[g] slots; some band uses all 64.
All inputs are finite; a program needn't handle non-finite values.
Results may differ from the reference program's by a relative error of at most 0.012.
The reference program's roundings to bfloat16 on the way (of `kernel` and `dft`) count: a program that leaves them out, or rounds other values in their place, can miss the bound.
Values sent between devices are 32-bit elements; how exact they have to be, the bound alone decides.
No kernel may reach another device: no remote copies, remote signals or barrier semaphores. Data moves between devices by JAX's collectives and lax.ppermute only.
A program may use at most 64 MiB of HBM per device.

```python
import jax
import jax.numpy as jnp
from jax import lax

PATCH = 128
SLICES = 4
TAPS = 33
CAP = 64
NC = 256
GROUPS = 64
GROUP_ROWS = 256
NR = 16384
NPOS = 4096


def draw_live_count(key, part):
    groups = NPOS // CAP
    counts = jax.random.randint(key, (groups,), CAP // 4, CAP + 1, dtype=jnp.int32)
    full_group = jax.random.randint(jax.random.fold_in(key, 1), (), 0, groups, dtype=jnp.int32)
    return jnp.where(jnp.arange(groups, dtype=jnp.int32) == full_group, CAP, counts).astype(jnp.int32)


def plant(drawn, rng, smallest, high):
    longest = drawn.shape.index(max(drawn.shape))
    spots = []
    for shift in (0, 1):
        where = [jax.random.randint(jax.random.fold_in(rng, axis), (), 0, length) for axis, length in enumerate(drawn.shape)]
        where[longest] = (where[longest] + shift) % drawn.shape[longest]
        spots.append(tuple(where))
    return drawn.at[spots[0]].set(smallest).at[spots[1]].set(high)


def level_of(key, shape, split, low, top_value):
    def one(dim, shards_of):
        heights = jax.random.uniform(jax.random.fold_in(jax.random.fold_in(key, 6), dim), (shards_of,), jnp.float32, low / len(split), top_value / len(split))
        return jnp.repeat(jnp.exp(heights), shape[dim] // shards_of).reshape((-1,) + (1,) * (len(shape) - dim - 1))

    factor_of = one(*split[0])
    for cut in split[1:]:
        factor_of = factor_of * one(*cut)
    return factor_of


def gaussian(own_key, shape, width, most, split=(), held_as=jnp.bfloat16):
    gain = level_of(own_key, shape, split, -0.22, 0.18) if split else 1.0
    array = jax.random.normal(own_key, shape, jnp.float32) * width * gain
    return jnp.minimum(jnp.maximum(array, -most), most).astype(held_as)


def setup_inputs(seed: int = 0) -> dict:
    splits = jax.random.split(jax.random.key(seed), 9)
    return {
        "obj_real": jnp.clip(1.0 + 0.1 * jax.random.normal(splits[0], (SLICES, NR, NC), jnp.float32), 0.5, 1.5),
        "obj_imag": gaussian(splits[1], (SLICES, NR, NC), 0.3, 4.0, ((1, 256),), jnp.float32),
        "probe": gaussian(splits[2], (2, PATCH, PATCH), 1.0, 6.0, (), jnp.float32),
        "fresnel_phase": jnp.clip(jax.random.uniform(splits[3], (TAPS,), jnp.float32, -3.140625, 3.140625), -3.140625, 3.140625),
        "row_offset": plant(jax.random.randint(splits[4], (NPOS,), 0, GROUP_ROWS), jax.random.fold_in(splits[4], 1), 0, GROUP_ROWS - 1).astype(jnp.int32),
        "col_offset": plant(jax.random.randint(splits[5], (NPOS,), 0, NC - PATCH + 1), jax.random.fold_in(splits[5], 1), 0, NC - PATCH).astype(jnp.int32),
        "live_count": draw_live_count(jax.random.fold_in(splits[8], 71), 0),
        "measured": jnp.clip(0.19921875 + 1.8007812 * jax.random.uniform(splits[7], (NPOS, PATCH, PATCH), jnp.float32) ** level_of(splits[7], (NPOS, PATCH, PATCH), ((0, 64),), -0.2, 0.2), 0.19921875, 2.0).astype(jnp.bfloat16),
    }


AMP_FLOOR = 0.25

def half_dot(left, right):
    return jnp.dot(left.astype(jnp.bfloat16), right.astype(jnp.bfloat16), preferred_element_type=jnp.float32)

def complex_dot(left, right):
    real = half_dot(left[0], right[0]) - half_dot(left[1], right[1])
    imag = half_dot(left[0], right[1]) + half_dot(left[1], right[0])
    return (real, imag)

def two_sided(matrix, wave):
    inner = complex_dot(matrix, wave)
    return complex_dot(inner, (matrix[0].T, matrix[1].T))

def tables(phase, patch):
    taps = phase.shape[0]
    rows = jnp.arange(patch, dtype=jnp.int32)[:, None]
    cols = jnp.arange(patch, dtype=jnp.int32)[None, :]
    offset = cols - rows + taps // 2
    picked = (offset[:, :, None] == jnp.arange(taps, dtype=jnp.int32)[None, None, :]).astype(phase.dtype)
    scale = 1.0 / jnp.sqrt(jnp.asarray(taps, phase.dtype))
    kern_re = (lax.optimization_barrier(jnp.sum(picked * jnp.cos(phase), axis=-1)) * scale).astype(jnp.bfloat16)
    kern_im = (lax.optimization_barrier(jnp.sum(picked * jnp.sin(phase), axis=-1)) * scale).astype(jnp.bfloat16)
    product = rows * cols % patch
    angle = 2.0 * jnp.pi / patch * product.astype(phase.dtype)
    norm = 1.0 / jnp.sqrt(jnp.asarray(patch, phase.dtype))
    dft_re = (jnp.cos(angle) * norm).astype(jnp.bfloat16)
    dft_im = (-jnp.sin(angle) * norm).astype(jnp.bfloat16)
    return ((kern_re, kern_im), (dft_re, dft_im))

def exit_loss(piece_re, piece_im, probe, target, weight, kernel, dft):
    wave_re, wave_im = (probe[0], probe[1])
    slices = piece_re.shape[0]
    for layer in range(slices):
        o_re, o_im = (piece_re[layer], piece_im[layer])
        wave_re, wave_im = (wave_re * o_re - wave_im * o_im, wave_re * o_im + wave_im * o_re)
        if layer + 1 < slices:
            wave_re, wave_im = two_sided(kernel, (wave_re, wave_im))
    far_re, far_im = two_sided(dft, (wave_re, wave_im))
    amplitude = jnp.sqrt(far_re * far_re + far_im * far_im + AMP_FLOOR)
    return 0.5 * weight * jnp.sum((amplitude - target) ** 2)

def reference(obj_real, obj_imag, probe, fresnel_phase, row_offset, col_offset, live_count, measured):
    kernel, dft = tables(fresnel_phase, PATCH)
    spare = jnp.zeros((SLICES, PATCH, NC), obj_real.dtype)
    ext_re = jnp.concatenate([obj_real, spare], axis=1)
    ext_im = jnp.concatenate([obj_imag, spare], axis=1)
    targets_all = measured.astype(jnp.float32)
    zero = jnp.zeros((), jnp.int32)
    grad_many = jax.vmap(jax.grad(exit_loss, argnums=(0, 1)), in_axes=(0, 0, None, 0, 0, None, None))

    def cut(field, top, left):
        return lax.dynamic_slice(field, (zero, top, left), (SLICES, PATCH, PATCH))

    def per_group(carry, group):
        first = group * CAP
        tops = group * GROUP_ROWS + lax.dynamic_slice_in_dim(row_offset, first, CAP)
        lefts = lax.dynamic_slice_in_dim(col_offset, first, CAP)
        targets = lax.dynamic_slice_in_dim(targets_all, first, CAP)
        live = lax.dynamic_index_in_dim(live_count, group, keepdims=False)
        weights = (jnp.arange(CAP, dtype=jnp.int32) < live).astype(obj_real.dtype)
        pieces_re = jax.vmap(cut, in_axes=(None, 0, 0))(ext_re, tops, lefts)
        pieces_im = jax.vmap(cut, in_axes=(None, 0, 0))(ext_im, tops, lefts)
        grads_re, grads_im = grad_many(pieces_re, pieces_im, probe, targets, weights, kernel, dft)

        def add_one(acc, item):
            top, left, one_re, one_im = item
            acc_re = lax.dynamic_update_slice(acc[0], cut(acc[0], top, left) + one_re, (zero, top, left))
            acc_im = lax.dynamic_update_slice(acc[1], cut(acc[1], top, left) + one_im, (zero, top, left))
            return ((acc_re, acc_im), None)
        carry, _ = lax.scan(add_one, carry, (tops, lefts, grads_re, grads_im))
        return (carry, None)
    start = (jnp.zeros_like(ext_re), jnp.zeros_like(ext_im))
    (acc_re, acc_im), _ = lax.scan(per_group, start, jnp.arange(GROUPS, dtype=jnp.int32))
    return (acc_re[:, :NR], acc_im[:, :NR])
```

```python
import jax
import jax.numpy as jnp
from jax import lax
from jax.experimental import pallas as pl
from jax.experimental.pallas import tpu as pltpu
from jax.sharding import PartitionSpec as P

AMP_FLOOR = 0.25
PATCH = 128
SLICES = 4
SHARD = 64
WINDOW = 3 * SHARD
CAP = 64
GROUP = 2
AXES = ("tile", "pos")


def kernel_table(phase):
    taps = phase.shape[0]
    rows = jnp.arange(PATCH, dtype=jnp.int32)[:, None]
    cols = jnp.arange(PATCH, dtype=jnp.int32)[None, :]
    offset = cols - rows + taps // 2
    picked = (offset[:, :, None] == jnp.arange(taps, dtype=jnp.int32)[None, None, :]).astype(
        phase.dtype
    )
    scale = 1.0 / jnp.sqrt(jnp.asarray(taps, phase.dtype))
    kern_re = (jnp.sum(picked * jnp.cos(phase), axis=-1) * scale).astype(jnp.bfloat16)
    kern_im = (jnp.sum(picked * jnp.sin(phase), axis=-1) * scale).astype(jnp.bfloat16)
    return kern_re, kern_im


def dft_table(dtype):
    rows = jnp.arange(PATCH, dtype=jnp.int32)[:, None]
    cols = jnp.arange(PATCH, dtype=jnp.int32)[None, :]
    product = rows * cols % PATCH
    angle = 2.0 * jnp.pi / PATCH * product.astype(dtype)
    norm = 1.0 / jnp.sqrt(jnp.asarray(PATCH, dtype))
    return (jnp.cos(angle) * norm).astype(jnp.bfloat16), (-jnp.sin(angle) * norm).astype(
        jnp.bfloat16
    )


def left_form(re, im):
    return jnp.block([[re, -im], [im, re]])


def stacked_tables(phase):
    left_k = left_form(*kernel_table(phase))
    left_d = left_form(*dft_table(phase.dtype))
    return jnp.stack([left_k, left_k.T, left_d, left_d.T])


def dot(a, b):
    return jnp.dot(a, b, preferred_element_type=jnp.float32)


def half(x):
    return x.astype(jnp.bfloat16)


def lanes_to_rows(wide):
    re = [wide[j * PATCH : (j + 1) * PATCH, :PATCH] for j in range(GROUP)]
    im = [wide[j * PATCH : (j + 1) * PATCH, PATCH:] for j in range(GROUP)]
    return jnp.concatenate(
        [jnp.concatenate(re, axis=1), jnp.concatenate(im, axis=1)], axis=0
    )


def rows_to_lanes(tall):
    return jnp.concatenate(
        [
            jnp.concatenate(
                [
                    tall[:PATCH, j * PATCH : (j + 1) * PATCH],
                    tall[PATCH:, j * PATCH : (j + 1) * PATCH],
                ],
                axis=1,
            )
            for j in range(GROUP)
        ],
        axis=0,
    )


def body(
    row_ref,
    col_ref,
    place_ref,
    probe_ref,
    table_ref,
    measured_hbm,
    own_hbm,
    via_a_hbm,
    via_b_hbm,
    via_c_hbm,
    send_a_hbm,
    send_b_hbm,
    middle_hbm,
    field,
    total,
    measured,
    wave_save,
    piece_save,
    slots,
    in_sem,
    out_sem,
    measured_sem,
):
    member = place_ref[0]
    live = place_ref[1]
    odd = (member % 2) == 1
    mine = (member + 3) % 4

    def window(ref, third):
        return ref.at[:, :, pl.ds(third * SHARD, SHARD), :]

    load_measured = pltpu.make_async_copy(measured_hbm, measured, measured_sem)
    load_measured.start()
    first = jnp.where(odd, 0, 2)
    load_a = pltpu.make_async_copy(via_a_hbm, window(field, first), in_sem.at[0])
    load_b = pltpu.make_async_copy(via_b_hbm, window(field, 2 - first), in_sem.at[1])
    load_own = pltpu.make_async_copy(own_hbm, window(field, 1), in_sem.at[2])
    load_c = pltpu.make_async_copy(via_c_hbm, window(field, 1), in_sem.at[2])
    load_a.start()
    load_b.start()

    @pl.when(member == 0)
    def _():
        load_c.start()

    @pl.when(member != 0)
    def _():
        load_own.start()

    def list_one(slot, count):
        slots[count] = slot
        hit = jnp.logical_and(slot < live, row_ref[slot] // SHARD == mine)
        return count + hit.astype(jnp.int32)

    count = lax.fori_loop(0, CAP, list_one, jnp.int32(0), unroll=8)
    for spare in range(GROUP):
        slots[count + spare] = 0

    for part in range(2):
        for layer in range(SLICES):
            total[part, layer] = jnp.zeros((WINDOW, 2 * PATCH), jnp.float32)

    load_a.wait()
    load_b.wait()
    load_own.wait()
    load_measured.wait()

    lane = lax.broadcasted_iota(jnp.int32, (1, 8, PATCH), 2)
    sub = lax.broadcasted_iota(jnp.int32, (1, 8, PATCH), 1)
    steps = PATCH // 8

    def cut(part, layer, base, rem, left):
        tall = field[part, layer, pl.ds(base, PATCH + 8), :]
        low = tall[:, :PATCH].reshape(steps + 1, 8, PATCH)
        high = tall[:, PATCH:].reshape(steps + 1, 8, PATCH)
        mixed = jnp.where(lane >= left, low, high)
        mixed = pltpu.roll(mixed, (PATCH - left) % PATCH, axis=2)
        mixed = pltpu.roll(mixed, (8 - rem) % 8, axis=1)
        return jnp.where(sub < 8 - rem, mixed[:-1], mixed[1:]).reshape(PATCH, PATCH)

    def add_back(part, layer, base, rem, left, value):
        value = value.reshape(steps, 8, PATCH)
        value = pltpu.roll(value, rem, axis=1)
        value = pltpu.roll(value, left % PATCH, axis=2)
        zero = jnp.zeros((1, 8, PATCH), jnp.float32)
        above = jnp.concatenate([value, zero], axis=0)
        below = jnp.concatenate([zero, value], axis=0)
        tall = jnp.where(sub >= rem, above, below)
        low = jnp.where(lane >= left, tall, 0.0).reshape(PATCH + 8, PATCH)
        high = jnp.where(lane < left, tall, 0.0).reshape(PATCH + 8, PATCH)
        total[part, layer, pl.ds(base, PATCH + 8), :PATCH] += low
        total[part, layer, pl.ds(base, PATCH + 8), PATCH:] += high

    def group_step(step, carry):
        where = []
        for j in range(GROUP):
            item = step * GROUP + j
            slot = slots[item]
            row = row_ref[slot] % SHARD
            left = col_ref[slot]
            base = pl.multiple_of((row // 8) * 8, 8)
            weight = (item < count).astype(jnp.float32)
            where.append((slot, base, row % 8, left, weight))

        left_k, right_k, left_d, right_d = [table_ref[i] for i in range(4)]
        wide = None
        for layer in range(SLICES):
            res, ims = [], []
            for j in range(GROUP):
                _, base, rem, left, _ = where[j]
                o_re = cut(0, layer, base, rem, left)
                o_im = cut(1, layer, base, rem, left)
                piece_save[0, layer, j] = o_re
                piece_save[1, layer, j] = o_im
                if layer == 0:
                    w_re, w_im = probe_ref[0], probe_ref[1]
                else:
                    w_re = wide[j * PATCH : (j + 1) * PATCH, :PATCH]
                    w_im = wide[j * PATCH : (j + 1) * PATCH, PATCH:]
                res.append(half(w_re * o_re - w_im * o_im))
                ims.append(half(w_re * o_im + w_im * o_re))
            tall = jnp.concatenate(
                [jnp.concatenate(res, axis=1), jnp.concatenate(ims, axis=1)], axis=0
            )
            last = layer + 1 == SLICES
            inner = half(dot(left_d if last else left_k, tall))
            wide = dot(rows_to_lanes(inner), right_d if last else right_k)
            if not last:
                wave_save[layer] = wide

        parts = []
        for j in range(GROUP):
            slot, _, _, _, weight = where[j]
            far_re = wide[j * PATCH : (j + 1) * PATCH, :PATCH]
            far_im = wide[j * PATCH : (j + 1) * PATCH, PATCH:]
            square = far_re * far_re + far_im * far_im + AMP_FLOOR
            target = measured[slot].astype(jnp.float32)
            scale = weight * (1.0 - target * lax.rsqrt(square))
            parts.append(jnp.concatenate([half(far_re * scale), half(far_im * scale)], axis=1))
        back = jnp.concatenate(parts, axis=0)
        for layer in range(SLICES - 1, -1, -1):
            last = layer + 1 == SLICES
            outer = half(dot(back, left_d if last else left_k))
            cot = dot(right_d if last else right_k, lanes_to_rows(outer))
            parts = []
            for j in range(GROUP):
                _, base, rem, left, _ = where[j]
                g_re = cot[:PATCH, j * PATCH : (j + 1) * PATCH]
                g_im = cot[PATCH:, j * PATCH : (j + 1) * PATCH]
                if layer == 0:
                    w_re, w_im = probe_ref[0], probe_ref[1]
                else:
                    w_re = wave_save[layer - 1, j * PATCH : (j + 1) * PATCH, :PATCH]
                    w_im = wave_save[layer - 1, j * PATCH : (j + 1) * PATCH, PATCH:]
                add_back(0, layer, base, rem, left, g_re * w_re + g_im * w_im)
                add_back(1, layer, base, rem, left, g_im * w_re - g_re * w_im)
                if layer > 0:
                    o_re = piece_save[0, layer, j]
                    o_im = piece_save[1, layer, j]
                    parts.append(
                        jnp.concatenate(
                            [half(g_re * o_re + g_im * o_im), half(g_im * o_re - g_re * o_im)],
                            axis=1,
                        )
                    )
            if layer > 0:
                back = jnp.concatenate(parts, axis=0)
        return carry

    lax.fori_loop(0, (count + GROUP - 1) // GROUP, group_step, jnp.int32(0))

    store_a = pltpu.make_async_copy(window(total, first), send_a_hbm, out_sem.at[0])
    store_b = pltpu.make_async_copy(window(total, 2 - first), send_b_hbm, out_sem.at[1])
    store_c = pltpu.make_async_copy(window(total, 1), middle_hbm, out_sem.at[2])
    store_a.start()
    store_b.start()
    store_c.start()
    store_a.wait()
    store_b.wait()
    store_c.wait()


def band_gradient(rows, cols, place, probe, tables, measured, own, via_a, via_b, via_c):
    smem = pl.BlockSpec(memory_space=pltpu.SMEM)
    vmem = pl.BlockSpec(memory_space=pltpu.VMEM)
    hbm = pl.BlockSpec(memory_space=pl.ANY)
    part = jax.ShapeDtypeStruct((2, SLICES, SHARD, 2 * PATCH), jnp.float32)
    whole = (2, SLICES, WINDOW, 2 * PATCH)
    return pl.pallas_call(
        body,
        out_shape=(part, part, part),
        in_specs=[smem, smem, smem, vmem, vmem, hbm, hbm, hbm, hbm, hbm],
        out_specs=(hbm, hbm, hbm),
        scratch_shapes=[
            pltpu.VMEM(whole, jnp.float32),
            pltpu.VMEM(whole, jnp.float32),
            pltpu.VMEM((CAP, PATCH, PATCH), jnp.bfloat16),
            pltpu.VMEM((SLICES - 1, GROUP * PATCH, 2 * PATCH), jnp.float32),
            pltpu.VMEM((2, SLICES, GROUP, PATCH, PATCH), jnp.float32),
            pltpu.SMEM((CAP + GROUP,), jnp.int32),
            pltpu.SemaphoreType.DMA((3,)),
            pltpu.SemaphoreType.DMA((3,)),
            pltpu.SemaphoreType.DMA,
        ],
        compiler_params=pltpu.CompilerParams(vmem_limit_bytes=40 * 1024 * 1024),
        cost_estimate=pl.CostEstimate(
            flops=5_000_000_000, bytes_accessed=8_000_000, transcendentals=0
        ),
    )(rows, cols, place, probe, tables, measured, own, via_a, via_b, via_c)


def route_pairs(tiles):
    via_a, via_b, via_c = [], [], []
    for t in range(tiles):
        at = 4 * t
        via_a += [(at, at + 1), (at + 2, at + 3), (at + 3, at + 2)]
        via_b += [(at + 1, at + 2), (at + 2, at + 1), (at + 3, at)]
        if t > 0:
            via_a.append((at + 1, at - 4))
            via_b.append((at, at - 1))
            via_c.append((at, at - 4))
    return via_a, via_b, via_c


def flipped(pairs):
    return [(b, a) for a, b in pairs]


def local(obj_real, obj_imag, probe, fresnel_phase, row_offset, col_offset, live_count, measured):
    via_a, via_b, via_c = route_pairs(lax.axis_size("tile"))
    own = jnp.stack([obj_real, obj_imag])
    got_c = lax.ppermute(own, AXES, via_c)
    got_a = lax.ppermute(own, AXES, via_a)
    got_b = lax.ppermute(own, AXES, via_b)
    member = lax.axis_index("pos").astype(jnp.int32)
    place = jnp.stack([member, live_count[0]])
    tables = stacked_tables(fresnel_phase)
    send_a, send_b, middle = band_gradient(
        row_offset, col_offset, place, probe, tables, measured, own, got_a, got_b, got_c
    )
    back_c = lax.ppermute(middle, AXES, flipped(via_c))
    back_a = lax.ppermute(send_a, AXES, flipped(via_a))
    back_b = lax.ppermute(send_b, AXES, flipped(via_b))
    out = back_a + back_b + jnp.where(member == 0, back_c, middle)
    return out[0], out[1]


def solution(mesh):
    rows = P(None, AXES, None)
    in_specs = (rows, rows, P(), P(), P("tile"), P("tile"), P("tile"), P("tile", None, None))
    return jax.shard_map(
        local, mesh=mesh, in_specs=in_specs, out_specs=(rows, rows), check_vma=False
    )
```

```python
import jax
import jax.numpy as jnp
import numpy as np
from jax import lax
from jax.experimental import pallas as pl
from jax.experimental.pallas import tpu as pltpu
from jax.sharding import PartitionSpec as P

AMP_FLOOR = 0.25
PATCH = 128
SLICES = 4
SHARD = 64
WINDOW = 3 * SHARD
CAP = 64
GROUP = 8
TAIL = 4
AXES = ("tile", "pos")


def kernel_table(phase):
    taps = phase.shape[0]
    rows = jnp.arange(PATCH, dtype=jnp.int32)[:, None]
    cols = jnp.arange(PATCH, dtype=jnp.int32)[None, :]
    offset = cols - rows + taps // 2
    picked = (offset[:, :, None] == jnp.arange(taps, dtype=jnp.int32)[None, None, :]).astype(
        phase.dtype
    )
    scale = 1.0 / jnp.sqrt(jnp.asarray(taps, phase.dtype))
    kern_re = (jnp.sum(picked * jnp.cos(phase), axis=-1) * scale).astype(jnp.bfloat16)
    kern_im = (jnp.sum(picked * jnp.sin(phase), axis=-1) * scale).astype(jnp.bfloat16)
    return kern_re, kern_im


def dft_table():
    index = np.arange(PATCH, dtype=np.int32)
    product = index[:, None] * index[None, :] % PATCH
    angle = np.float32(2.0 * np.pi / PATCH) * product.astype(np.float32)
    norm = np.float32(1.0) / np.sqrt(np.float32(PATCH))
    return (np.cos(angle) * norm).astype(jnp.bfloat16), (-np.sin(angle) * norm).astype(jnp.bfloat16)


def stacked_tables(phase):
    re, im = kernel_table(phase)
    left_k = jnp.block([[re, -im], [im, re]])
    dft_re, dft_im = dft_table()
    left_d = np.block([[dft_re, -dft_im], [dft_im, dft_re]])
    return jnp.stack([left_k, left_k.T]), jnp.asarray(np.stack([left_d, left_d.T]))


def dot(a, b):
    return jnp.dot(a, b, preferred_element_type=jnp.float32)


def half(x):
    return x.astype(jnp.bfloat16)


def lanes_to_rows(wide, size):
    re = [wide[j * PATCH : (j + 1) * PATCH, :PATCH] for j in range(size)]
    im = [wide[j * PATCH : (j + 1) * PATCH, PATCH:] for j in range(size)]
    return jnp.concatenate(
        [jnp.concatenate(re, axis=1), jnp.concatenate(im, axis=1)], axis=0
    )


def rows_to_lanes(tall, size):
    return jnp.concatenate(
        [
            jnp.concatenate(
                [
                    tall[:PATCH, j * PATCH : (j + 1) * PATCH],
                    tall[PATCH:, j * PATCH : (j + 1) * PATCH],
                ],
                axis=1,
            )
            for j in range(size)
        ],
        axis=0,
    )


def body(
    row_ref,
    col_ref,
    place_ref,
    probe_ref,
    prop_ref,
    dft_ref,
    measured_hbm,
    own_hbm,
    via_a_hbm,
    via_b_hbm,
    via_c_hbm,
    send_a_hbm,
    send_b_hbm,
    middle_hbm,
    field,
    total,
    measured,
    wave_save,
    piece_save,
    slots,
    in_sem,
    out_sem,
    measured_sem,
):
    member = place_ref[0]
    live = place_ref[1]
    odd = (member % 2) == 1
    mine = (member + 3) % 4

    def window(ref, third):
        return ref.at[:, :, pl.ds(third * SHARD, SHARD), :]

    load_measured = pltpu.make_async_copy(measured_hbm, measured, measured_sem)
    load_measured.start()
    first = jnp.where(odd, 0, 2)
    load_a = pltpu.make_async_copy(via_a_hbm, window(field, first), in_sem.at[0])
    load_b = pltpu.make_async_copy(via_b_hbm, window(field, 2 - first), in_sem.at[1])
    load_own = pltpu.make_async_copy(own_hbm, window(field, 1), in_sem.at[2])
    load_c = pltpu.make_async_copy(via_c_hbm, window(field, 1), in_sem.at[2])
    load_a.start()
    load_b.start()

    @pl.when(member == 0)
    def _():
        load_c.start()

    @pl.when(member != 0)
    def _():
        load_own.start()

    def list_one(slot, count):
        slots[count] = slot
        hit = jnp.logical_and(slot < live, row_ref[slot] // SHARD == mine)
        return count + hit.astype(jnp.int32)

    count = lax.fori_loop(0, CAP, list_one, jnp.int32(0), unroll=8)
    for spare in range(GROUP):
        slots[count + spare] = 0

    for part in range(2):
        for layer in range(SLICES):
            total[part, layer] = jnp.zeros((WINDOW, 2 * PATCH), jnp.float32)

    load_a.wait()
    load_b.wait()
    load_own.wait()
    load_measured.wait()

    lane = lax.broadcasted_iota(jnp.int32, (1, 8, PATCH), 2)
    sub = lax.broadcasted_iota(jnp.int32, (1, 8, PATCH), 1)
    steps = PATCH // 8

    def cut(part, layer, base, rem, left):
        tall = field[part, layer, pl.ds(base, PATCH + 8), :]
        low = tall[:, :PATCH].reshape(steps + 1, 8, PATCH)
        high = tall[:, PATCH:].reshape(steps + 1, 8, PATCH)
        mixed = jnp.where(lane >= left, low, high)
        mixed = pltpu.roll(mixed, (PATCH - left) % PATCH, axis=2)
        mixed = pltpu.roll(mixed, (8 - rem) % 8, axis=1)
        return jnp.where(sub < 8 - rem, mixed[:-1], mixed[1:]).reshape(PATCH, PATCH)

    def add_back(part, layer, base, rem, left, value):
        value = value.reshape(steps, 8, PATCH)
        value = pltpu.roll(value, rem, axis=1)
        value = pltpu.roll(value, left % PATCH, axis=2)
        zero = jnp.zeros((1, 8, PATCH), jnp.float32)
        above = jnp.concatenate([value, zero], axis=0)
        below = jnp.concatenate([zero, value], axis=0)
        tall = jnp.where(sub >= rem, above, below)
        low = jnp.where(lane >= left, tall, 0.0).reshape(PATCH + 8, PATCH)
        high = jnp.where(lane < left, tall, 0.0).reshape(PATCH + 8, PATCH)
        total[part, layer, pl.ds(base, PATCH + 8), :PATCH] += low
        total[part, layer, pl.ds(base, PATCH + 8), PATCH:] += high

    def group(start, size):
        where = []
        for j in range(size):
            item = start + j
            slot = slots[item]
            row = row_ref[slot] % SHARD
            left = col_ref[slot]
            base = pl.multiple_of((row // 8) * 8, 8)
            weight = (item < count).astype(jnp.float32)
            where.append((slot, base, row % 8, left, weight))

        left_k, right_k = prop_ref[0], prop_ref[1]
        left_d, right_d = dft_ref[0], dft_ref[1]
        wide = None
        for layer in range(SLICES):
            res, ims = [], []
            for j in range(size):
                _, base, rem, left, _ = where[j]
                o_re = cut(0, layer, base, rem, left)
                o_im = cut(1, layer, base, rem, left)
                if layer > 0:
                    piece_save[0, layer - 1, j] = o_re
                    piece_save[1, layer - 1, j] = o_im
                if layer == 0:
                    w_re, w_im = probe_ref[0], probe_ref[1]
                else:
                    w_re = wide[j * PATCH : (j + 1) * PATCH, :PATCH]
                    w_im = wide[j * PATCH : (j + 1) * PATCH, PATCH:]
                res.append(half(w_re * o_re - w_im * o_im))
                ims.append(half(w_re * o_im + w_im * o_re))
            tall = jnp.concatenate(
                [jnp.concatenate(res, axis=1), jnp.concatenate(ims, axis=1)], axis=0
            )
            last = layer + 1 == SLICES
            inner = half(dot(left_d if last else left_k, tall))
            wide = dot(rows_to_lanes(inner, size), right_d if last else right_k)
            if not last:
                wave_save[layer, : size * PATCH] = wide

        parts = []
        for j in range(size):
            slot, _, _, _, weight = where[j]
            far_re = wide[j * PATCH : (j + 1) * PATCH, :PATCH]
            far_im = wide[j * PATCH : (j + 1) * PATCH, PATCH:]
            square = far_re * far_re + far_im * far_im + AMP_FLOOR
            target = measured[slot].astype(jnp.float32)
            scale = weight * (1.0 - target * lax.rsqrt(square))
            parts.append(jnp.concatenate([half(far_re * scale), half(far_im * scale)], axis=1))
        back = jnp.concatenate(parts, axis=0)
        for layer in range(SLICES - 1, -1, -1):
            last = layer + 1 == SLICES
            outer = half(dot(back, left_d if last else left_k))
            cot = dot(right_d if last else right_k, lanes_to_rows(outer, size))
            parts = []
            for j in range(size):
                _, base, rem, left, _ = where[j]
                g_re = cot[:PATCH, j * PATCH : (j + 1) * PATCH]
                g_im = cot[PATCH:, j * PATCH : (j + 1) * PATCH]
                if layer == 0:
                    w_re, w_im = probe_ref[0], probe_ref[1]
                else:
                    w_re = wave_save[layer - 1, j * PATCH : (j + 1) * PATCH, :PATCH]
                    w_im = wave_save[layer - 1, j * PATCH : (j + 1) * PATCH, PATCH:]
                add_back(0, layer, base, rem, left, g_re * w_re + g_im * w_im)
                add_back(1, layer, base, rem, left, g_im * w_re - g_re * w_im)
                if layer > 0:
                    o_re = piece_save[0, layer - 1, j]
                    o_im = piece_save[1, layer - 1, j]
                    parts.append(
                        jnp.concatenate(
                            [half(g_re * o_re + g_im * o_im), half(g_im * o_re - g_re * o_im)],
                            axis=1,
                        )
                    )
            if layer > 0:
                back = jnp.concatenate(parts, axis=0)

    def full_step(step, carry):
        group(step * GROUP, GROUP)
        return carry

    rest = count % GROUP
    steps_full = count // GROUP + (rest > TAIL).astype(jnp.int32)
    lax.fori_loop(0, steps_full, full_step, jnp.int32(0))

    @pl.when(jnp.logical_and(rest > 0, rest <= TAIL))
    def _():
        group(steps_full * GROUP, TAIL)

    store_a = pltpu.make_async_copy(window(total, first), send_a_hbm, out_sem.at[0])
    store_b = pltpu.make_async_copy(window(total, 2 - first), send_b_hbm, out_sem.at[1])
    store_c = pltpu.make_async_copy(window(total, 1), middle_hbm, out_sem.at[2])
    store_a.start()
    store_b.start()
    store_c.start()
    store_a.wait()
    store_b.wait()
    store_c.wait()


def band_gradient(rows, cols, place, probe, tables, measured, own, via_a, via_b, via_c):
    smem = pl.BlockSpec(memory_space=pltpu.SMEM)
    vmem = pl.BlockSpec(memory_space=pltpu.VMEM)
    hbm = pl.BlockSpec(memory_space=pltpu.HBM)
    part = jax.ShapeDtypeStruct((2, SLICES, SHARD, 2 * PATCH), jnp.float32)
    whole = (2, SLICES, WINDOW, 2 * PATCH)
    return pl.pallas_call(
        body,
        out_shape=(part, part, part),
        in_specs=[smem, smem, smem, vmem, vmem, vmem, hbm, hbm, hbm, hbm, hbm],
        out_specs=(hbm, hbm, hbm),
        scratch_shapes=[
            pltpu.VMEM(whole, jnp.float32),
            pltpu.VMEM(whole, jnp.float32),
            pltpu.VMEM((CAP, PATCH, PATCH), jnp.bfloat16),
            pltpu.VMEM((SLICES - 1, GROUP * PATCH, 2 * PATCH), jnp.float32),
            pltpu.VMEM((2, SLICES - 1, GROUP, PATCH, PATCH), jnp.float32),
            pltpu.SMEM((CAP + GROUP,), jnp.int32),
            pltpu.SemaphoreType.DMA((3,)),
            pltpu.SemaphoreType.DMA((3,)),
            pltpu.SemaphoreType.DMA,
        ],
        compiler_params=pltpu.CompilerParams(vmem_limit_bytes=48 * 1024 * 1024),
        cost_estimate=pl.CostEstimate(
            flops=5_000_000_000, bytes_accessed=8_000_000, transcendentals=0
        ),
    )(rows, cols, place, probe, *tables, measured, own, via_a, via_b, via_c)


def route_pairs(tiles):
    via_a, via_b, via_c = [], [], []
    for t in range(tiles):
        at = 4 * t
        via_a += [(at, at + 1), (at + 2, at + 3), (at + 3, at + 2)]
        via_b += [(at + 1, at + 2), (at + 2, at + 1), (at + 3, at)]
        if t > 0:
            via_a.append((at + 1, at - 4))
            via_b.append((at, at - 1))
            via_c.append((at, at - 4))
    return via_a, via_b, via_c


def flipped(pairs):
    return [(b, a) for a, b in pairs]


def local(obj_real, obj_imag, probe, fresnel_phase, row_offset, col_offset, live_count, measured):
    via_a, via_b, via_c = route_pairs(lax.axis_size("tile"))
    own = jnp.stack([obj_real, obj_imag])
    got_c = lax.ppermute(own, AXES, via_c)
    got_a = lax.ppermute(own, AXES, via_a)
    got_b = lax.ppermute(own, AXES, via_b)
    member = lax.axis_index("pos").astype(jnp.int32)
    place = jnp.stack([member, live_count[0]])
    tables = stacked_tables(fresnel_phase)
    send_a, send_b, middle = band_gradient(
        row_offset, col_offset, place, probe, tables, measured, own, got_a, got_b, got_c
    )
    back_c = lax.ppermute(middle, AXES, flipped(via_c))
    back_a = lax.ppermute(send_a, AXES, flipped(via_a))
    back_b = lax.ppermute(send_b, AXES, flipped(via_b))
    out = back_a + back_b + jnp.where(member == 0, back_c, middle)
    return out[0], out[1]


def solution(mesh):
    rows = P(None, AXES, None)
    in_specs = (rows, rows, P(), P(), P("tile"), P("tile"), P("tile"), P("tile", None, None))
    return jax.shard_map(
        local, mesh=mesh, in_specs=in_specs, out_specs=(rows, rows), check_vma=False
    )
```

```python
import jax
import jax.numpy as jnp
import numpy as np
from jax import lax
from jax.experimental import pallas as pl
from jax.experimental.pallas import tpu as pltpu
from jax.sharding import PartitionSpec as P

AMP_FLOOR = 0.25
PATCH = 128
SLICES = 4
SHARD = 64
WINDOW = 3 * SHARD
CAP = 64
GROUP = 8
TAIL = 4
AXES = ("tile", "pos")


def kernel_table(phase):
    taps = phase.shape[0]
    rows = jnp.arange(PATCH, dtype=jnp.int32)[:, None]
    cols = jnp.arange(PATCH, dtype=jnp.int32)[None, :]
    offset = cols - rows + taps // 2
    picked = (offset[:, :, None] == jnp.arange(taps, dtype=jnp.int32)[None, None, :]).astype(
        phase.dtype
    )
    scale = 1.0 / jnp.sqrt(jnp.asarray(taps, phase.dtype))
    kern_re = (jnp.sum(picked * jnp.cos(phase), axis=-1) * scale).astype(jnp.bfloat16)
    kern_im = (jnp.sum(picked * jnp.sin(phase), axis=-1) * scale).astype(jnp.bfloat16)
    return kern_re, kern_im


def dft_table():
    index = np.arange(PATCH, dtype=np.int32)
    product = index[:, None] * index[None, :] % PATCH
    angle = np.float32(2.0 * np.pi / PATCH) * product.astype(np.float32)
    norm = np.float32(1.0) / np.sqrt(np.float32(PATCH))
    return (np.cos(angle) * norm).astype(jnp.bfloat16), (-np.sin(angle) * norm).astype(jnp.bfloat16)


def stacked_tables(phase):
    re, im = kernel_table(phase)
    left_k = jnp.block([[re, -im], [im, re]])
    dft_re, dft_im = dft_table()
    left_d = np.block([[dft_re, -dft_im], [dft_im, dft_re]])
    return jnp.stack([left_k, left_k.T]), jnp.asarray(np.stack([left_d, left_d.T]))


def dot(a, b):
    return jnp.dot(a, b, preferred_element_type=jnp.float32)


def half(x):
    return x.astype(jnp.bfloat16)


def lanes_to_rows(wide, size):
    re = [wide[j * PATCH : (j + 1) * PATCH, :PATCH] for j in range(size)]
    im = [wide[j * PATCH : (j + 1) * PATCH, PATCH:] for j in range(size)]
    return jnp.concatenate(
        [jnp.concatenate(re, axis=1), jnp.concatenate(im, axis=1)], axis=0
    )


def rows_to_lanes(tall, size):
    return jnp.concatenate(
        [
            jnp.concatenate(
                [
                    tall[:PATCH, j * PATCH : (j + 1) * PATCH],
                    tall[PATCH:, j * PATCH : (j + 1) * PATCH],
                ],
                axis=1,
            )
            for j in range(size)
        ],
        axis=0,
    )


def body(
    row_ref,
    col_ref,
    place_ref,
    probe_ref,
    prop_ref,
    dft_ref,
    measured_hbm,
    own_hbm,
    across_hbm,
    below_hbm,
    above_hbm,
    send_up_hbm,
    send_down_hbm,
    middle_hbm,
    field,
    total,
    measured,
    wave_save,
    piece_save,
    slots,
    in_sem,
    out_sem,
    measured_sem,
):
    member = place_ref[0]
    live = place_ref[1]
    mine = (member + 3) % 4

    def window(ref, third):
        return ref.at[:, :, pl.ds(third * SHARD, SHARD), :]

    load_measured = pltpu.make_async_copy(measured_hbm, measured, measured_sem)
    load_measured.start()
    load_a = pltpu.make_async_copy(above_hbm, window(field, 0), in_sem.at[0])
    load_b = pltpu.make_async_copy(below_hbm, window(field, 2), in_sem.at[1])
    load_own = pltpu.make_async_copy(own_hbm, window(field, 1), in_sem.at[2])
    load_c = pltpu.make_async_copy(across_hbm, window(field, 1), in_sem.at[2])
    load_a.start()
    load_b.start()

    @pl.when(member == 0)
    def _():
        load_c.start()

    @pl.when(member != 0)
    def _():
        load_own.start()

    def list_one(slot, count):
        slots[count] = slot
        hit = jnp.logical_and(slot < live, row_ref[slot] // SHARD == mine)
        return count + hit.astype(jnp.int32)

    count = lax.fori_loop(0, CAP, list_one, jnp.int32(0), unroll=8)
    for spare in range(GROUP):
        slots[count + spare] = 0

    for part in range(2):
        for layer in range(SLICES):
            total[part, layer] = jnp.zeros((WINDOW, 2 * PATCH), jnp.float32)

    load_a.wait()
    load_b.wait()
    load_own.wait()
    load_measured.wait()

    lane = lax.broadcasted_iota(jnp.int32, (1, 8, PATCH), 2)
    sub = lax.broadcasted_iota(jnp.int32, (1, 8, PATCH), 1)
    steps = PATCH // 8

    def cut(part, layer, base, rem, left):
        tall = field[part, layer, pl.ds(base, PATCH + 8), :]
        low = tall[:, :PATCH].reshape(steps + 1, 8, PATCH)
        high = tall[:, PATCH:].reshape(steps + 1, 8, PATCH)
        mixed = jnp.where(lane >= left, low, high)
        mixed = pltpu.roll(mixed, (PATCH - left) % PATCH, axis=2)
        mixed = pltpu.roll(mixed, (8 - rem) % 8, axis=1)
        return jnp.where(sub < 8 - rem, mixed[:-1], mixed[1:]).reshape(PATCH, PATCH)

    def add_back(part, layer, base, rem, left, value):
        value = value.reshape(steps, 8, PATCH)
        value = pltpu.roll(value, rem, axis=1)
        value = pltpu.roll(value, left % PATCH, axis=2)
        zero = jnp.zeros((1, 8, PATCH), jnp.float32)
        above = jnp.concatenate([value, zero], axis=0)
        below = jnp.concatenate([zero, value], axis=0)
        tall = jnp.where(sub >= rem, above, below)
        low = jnp.where(lane >= left, tall, 0.0).reshape(PATCH + 8, PATCH)
        high = jnp.where(lane < left, tall, 0.0).reshape(PATCH + 8, PATCH)
        total[part, layer, pl.ds(base, PATCH + 8), :PATCH] += low
        total[part, layer, pl.ds(base, PATCH + 8), PATCH:] += high

    def group(start, size):
        where = []
        for j in range(size):
            item = start + j
            slot = slots[item]
            row = row_ref[slot] % SHARD
            left = col_ref[slot]
            base = pl.multiple_of((row // 8) * 8, 8)
            weight = (item < count).astype(jnp.float32)
            where.append((slot, base, row % 8, left, weight))

        left_k, right_k = prop_ref[0], prop_ref[1]
        left_d, right_d = dft_ref[0], dft_ref[1]
        wide = None
        for layer in range(SLICES):
            res, ims = [], []
            for j in range(size):
                _, base, rem, left, _ = where[j]
                o_re = cut(0, layer, base, rem, left)
                o_im = cut(1, layer, base, rem, left)
                if layer > 0:
                    piece_save[0, layer - 1, j] = o_re
                    piece_save[1, layer - 1, j] = o_im
                if layer == 0:
                    w_re, w_im = probe_ref[0], probe_ref[1]
                else:
                    w_re = wide[j * PATCH : (j + 1) * PATCH, :PATCH]
                    w_im = wide[j * PATCH : (j + 1) * PATCH, PATCH:]
                res.append(half(w_re * o_re - w_im * o_im))
                ims.append(half(w_re * o_im + w_im * o_re))
            tall = jnp.concatenate(
                [jnp.concatenate(res, axis=1), jnp.concatenate(ims, axis=1)], axis=0
            )
            last = layer + 1 == SLICES
            inner = half(dot(left_d if last else left_k, tall))
            wide = dot(rows_to_lanes(inner, size), right_d if last else right_k)
            if not last:
                wave_save[layer, : size * PATCH] = wide

        parts = []
        for j in range(size):
            slot, _, _, _, weight = where[j]
            far_re = wide[j * PATCH : (j + 1) * PATCH, :PATCH]
            far_im = wide[j * PATCH : (j + 1) * PATCH, PATCH:]
            square = far_re * far_re + far_im * far_im + AMP_FLOOR
            target = measured[slot].astype(jnp.float32)
            scale = weight * (1.0 - target * lax.rsqrt(square))
            parts.append(jnp.concatenate([half(far_re * scale), half(far_im * scale)], axis=1))
        back = jnp.concatenate(parts, axis=0)
        for layer in range(SLICES - 1, -1, -1):
            last = layer + 1 == SLICES
            outer = half(dot(back, left_d if last else left_k))
            cot = dot(right_d if last else right_k, lanes_to_rows(outer, size))
            parts = []
            for j in range(size):
                _, base, rem, left, _ = where[j]
                g_re = cot[:PATCH, j * PATCH : (j + 1) * PATCH]
                g_im = cot[PATCH:, j * PATCH : (j + 1) * PATCH]
                if layer == 0:
                    w_re, w_im = probe_ref[0], probe_ref[1]
                else:
                    w_re = wave_save[layer - 1, j * PATCH : (j + 1) * PATCH, :PATCH]
                    w_im = wave_save[layer - 1, j * PATCH : (j + 1) * PATCH, PATCH:]
                add_back(0, layer, base, rem, left, g_re * w_re + g_im * w_im)
                add_back(1, layer, base, rem, left, g_im * w_re - g_re * w_im)
                if layer > 0:
                    o_re = piece_save[0, layer - 1, j]
                    o_im = piece_save[1, layer - 1, j]
                    parts.append(
                        jnp.concatenate(
                            [half(g_re * o_re + g_im * o_im), half(g_im * o_re - g_re * o_im)],
                            axis=1,
                        )
                    )
            if layer > 0:
                back = jnp.concatenate(parts, axis=0)

    def full_step(step, carry):
        group(step * GROUP, GROUP)
        return carry

    rest = count % GROUP
    steps_full = count // GROUP + (rest > TAIL).astype(jnp.int32)
    lax.fori_loop(0, steps_full, full_step, jnp.int32(0))

    @pl.when(jnp.logical_and(rest > 0, rest <= TAIL))
    def _():
        group(steps_full * GROUP, TAIL)

    store_a = pltpu.make_async_copy(window(total, 0), send_up_hbm, out_sem.at[0])
    store_b = pltpu.make_async_copy(window(total, 2), send_down_hbm, out_sem.at[1])
    store_c = pltpu.make_async_copy(window(total, 1), middle_hbm, out_sem.at[2])
    store_a.start()
    store_b.start()
    store_c.start()
    store_a.wait()
    store_b.wait()
    store_c.wait()


def band_gradient(rows, cols, place, probe, tables, measured, own, across, below, above):
    smem = pl.BlockSpec(memory_space=pltpu.SMEM)
    vmem = pl.BlockSpec(memory_space=pltpu.VMEM)
    hbm = pl.BlockSpec(memory_space=pltpu.HBM)
    part = jax.ShapeDtypeStruct((2, SLICES, SHARD, 2 * PATCH), jnp.float32)
    whole = (2, SLICES, WINDOW, 2 * PATCH)
    return pl.pallas_call(
        body,
        out_shape=(part, part, part),
        in_specs=[smem, smem, smem, vmem, vmem, vmem, hbm, hbm, hbm, hbm, hbm],
        out_specs=(hbm, hbm, hbm),
        scratch_shapes=[
            pltpu.VMEM(whole, jnp.float32),
            pltpu.VMEM(whole, jnp.float32),
            pltpu.VMEM((CAP, PATCH, PATCH), jnp.bfloat16),
            pltpu.VMEM((SLICES - 1, GROUP * PATCH, 2 * PATCH), jnp.float32),
            pltpu.VMEM((2, SLICES - 1, GROUP, PATCH, PATCH), jnp.float32),
            pltpu.SMEM((CAP + GROUP,), jnp.int32),
            pltpu.SemaphoreType.DMA((3,)),
            pltpu.SemaphoreType.DMA((3,)),
            pltpu.SemaphoreType.DMA,
        ],
        compiler_params=pltpu.CompilerParams(vmem_limit_bytes=48 * 1024 * 1024),
        cost_estimate=pl.CostEstimate(
            flops=5_000_000_000, bytes_accessed=8_000_000, transcendentals=0
        ),
    )(rows, cols, place, probe, *tables, measured, own, across, below, above)


def route_pairs(tiles):
    up, down, tile = [], [], []
    for t in range(tiles):
        at = 4 * t
        up += [(at, at + 1), (at + 1, at + 2), (at + 2, at + 3), (at + 3, at)]
        down += [(at + 2, at + 1), (at + 3, at + 2)]
        if t > 0:
            down += [(at, at - 1), (at + 1, at - 4)]
            tile.append((at, at - 4))
    return up, down, tile


def flipped(pairs):
    return [(b, a) for a, b in pairs]


def local(obj_real, obj_imag, probe, fresnel_phase, row_offset, col_offset, live_count, measured):
    up, down, tile = route_pairs(lax.axis_size("tile"))
    own = jnp.stack([obj_real, obj_imag])
    below = lax.ppermute(own, AXES, down)
    across = lax.ppermute(own, AXES, tile)
    above = lax.ppermute(own, AXES, up)
    member = lax.axis_index("pos").astype(jnp.int32)
    place = jnp.stack([member, live_count[0]])
    tables = stacked_tables(fresnel_phase)
    send_up, send_down, middle = band_gradient(
        row_offset, col_offset, place, probe, tables, measured, own, across, below, above
    )
    back_down = lax.ppermute(send_down, AXES, flipped(down))
    back_tile = lax.ppermute(middle, AXES, flipped(tile))
    back_up = lax.ppermute(send_up, AXES, flipped(up))

    def sum_of(part):
        mid = jnp.where(member == 0, back_tile[part], middle[part])
        return mid + back_down[part] + back_up[part]

    return sum_of(0), sum_of(1)


def solution(mesh):
    rows = P(None, AXES, None)
    in_specs = (rows, rows, P(), P(), P("tile"), P("tile"), P("tile"), P("tile", None, None))
    return jax.shard_map(
        local, mesh=mesh, in_specs=in_specs, out_specs=(rows, rows), check_vma=False
    )
```

```python
import jax
import jax.numpy as jnp
import numpy as np
from jax import lax
from jax.experimental import pallas as pl
from jax.experimental.pallas import tpu as pltpu
from jax.sharding import PartitionSpec as P

AMP_FLOOR = 0.25
PATCH = 128
SLICES = 4
SHARD = 64
WINDOW = 3 * SHARD
CAP = 64
GROUP = 8
TAIL = 4
AXES = ("tile", "pos")


def kernel_table(phase):
    taps = phase.shape[0]
    rows = jnp.arange(PATCH, dtype=jnp.int32)[:, None]
    cols = jnp.arange(PATCH, dtype=jnp.int32)[None, :]
    offset = cols - rows + taps // 2
    picked = (offset[:, :, None] == jnp.arange(taps, dtype=jnp.int32)[None, None, :]).astype(
        phase.dtype
    )
    scale = 1.0 / jnp.sqrt(jnp.asarray(taps, phase.dtype))
    kern_re = (jnp.sum(picked * jnp.cos(phase), axis=-1) * scale).astype(jnp.bfloat16)
    kern_im = (jnp.sum(picked * jnp.sin(phase), axis=-1) * scale).astype(jnp.bfloat16)
    return kern_re, kern_im


def dft_table():
    index = np.arange(PATCH, dtype=np.int32)
    product = index[:, None] * index[None, :] % PATCH
    angle = np.float32(2.0 * np.pi / PATCH) * product.astype(np.float32)
    norm = np.float32(1.0) / np.sqrt(np.float32(PATCH))
    return (np.cos(angle) * norm).astype(jnp.bfloat16), (-np.sin(angle) * norm).astype(jnp.bfloat16)


def stacked_tables(phase):
    re, im = kernel_table(phase)
    left_k = jnp.block([[re, -im], [im, re]])
    dft_re, dft_im = dft_table()
    left_d = np.block([[dft_re, -dft_im], [dft_im, dft_re]])
    return jnp.stack([left_k, left_k.T]), jnp.asarray(np.stack([left_d, left_d.T]))


def dot(a, b):
    return jnp.dot(a, b, preferred_element_type=jnp.float32)


def half(x):
    return x.astype(jnp.bfloat16)


def lanes_to_rows(wide, size):
    re = [wide[j * PATCH : (j + 1) * PATCH, :PATCH] for j in range(size)]
    im = [wide[j * PATCH : (j + 1) * PATCH, PATCH:] for j in range(size)]
    return jnp.concatenate(
        [jnp.concatenate(re, axis=1), jnp.concatenate(im, axis=1)], axis=0
    )


def rows_to_lanes(tall, size):
    return jnp.concatenate(
        [
            jnp.concatenate(
                [
                    tall[:PATCH, j * PATCH : (j + 1) * PATCH],
                    tall[PATCH:, j * PATCH : (j + 1) * PATCH],
                ],
                axis=1,
            )
            for j in range(size)
        ],
        axis=0,
    )


def body(
    row_ref,
    col_ref,
    place_ref,
    probe_ref,
    prop_ref,
    dft_ref,
    measured_hbm,
    own_hbm,
    across_hbm,
    below_hbm,
    above_hbm,
    send_up_hbm,
    send_down_hbm,
    middle_hbm,
    field,
    total,
    measured,
    wave_save,
    piece_save,
    slots,
    in_sem,
    out_sem,
    measured_sem,
):
    member = place_ref[0]
    live = place_ref[1]
    mine = (member + 3) % 4

    def window(ref, third):
        return ref.at[:, :, pl.ds(third * SHARD, SHARD), :]

    load_measured = pltpu.make_async_copy(measured_hbm, measured, measured_sem)
    load_measured.start()
    load_a = pltpu.make_async_copy(above_hbm, window(field, 0), in_sem.at[0])
    load_b = pltpu.make_async_copy(below_hbm, window(field, 2), in_sem.at[1])
    load_own = pltpu.make_async_copy(own_hbm, window(field, 1), in_sem.at[2])
    load_c = pltpu.make_async_copy(across_hbm, window(field, 1), in_sem.at[2])
    load_a.start()
    load_b.start()

    @pl.when(member == 0)
    def _():
        load_c.start()

    @pl.when(member != 0)
    def _():
        load_own.start()

    def list_one(slot, count):
        slots[count] = slot
        hit = jnp.logical_and(slot < live, row_ref[slot] // SHARD == mine)
        return count + hit.astype(jnp.int32)

    count = lax.fori_loop(0, CAP, list_one, jnp.int32(0), unroll=8)
    for spare in range(GROUP):
        slots[count + spare] = 0

    for part in range(2):
        for layer in range(SLICES):
            total[part, layer] = jnp.zeros((WINDOW, 2 * PATCH), jnp.float32)

    load_a.wait()
    load_b.wait()
    load_own.wait()
    load_measured.wait()

    lane = lax.broadcasted_iota(jnp.int32, (1, 8, PATCH), 2)
    sub = lax.broadcasted_iota(jnp.int32, (1, 8, PATCH), 1)
    steps = PATCH // 8

    def cut(part, layer, base, rem, left):
        tall = field[part, layer, pl.ds(base, PATCH + 8), :]
        low = tall[:, :PATCH].reshape(steps + 1, 8, PATCH)
        high = tall[:, PATCH:].reshape(steps + 1, 8, PATCH)
        mixed = jnp.where(lane >= left, low, high)
        mixed = pltpu.roll(mixed, (PATCH - left) % PATCH, axis=2)
        mixed = pltpu.roll(mixed, (8 - rem) % 8, axis=1)
        return jnp.where(sub < 8 - rem, mixed[:-1], mixed[1:]).reshape(PATCH, PATCH)

    def add_back(part, layer, base, rem, left, value):
        value = value.reshape(steps, 8, PATCH)
        value = pltpu.roll(value, rem, axis=1)
        value = pltpu.roll(value, left % PATCH, axis=2)
        zero = jnp.zeros((1, 8, PATCH), jnp.float32)
        above = jnp.concatenate([value, zero], axis=0)
        below = jnp.concatenate([zero, value], axis=0)
        tall = jnp.where(sub >= rem, above, below)
        low = jnp.where(lane >= left, tall, 0.0).reshape(PATCH + 8, PATCH)
        high = jnp.where(lane < left, tall, 0.0).reshape(PATCH + 8, PATCH)
        total[part, layer, pl.ds(base, PATCH + 8), :PATCH] += low
        total[part, layer, pl.ds(base, PATCH + 8), PATCH:] += high

    def group(start, size):
        where = []
        for j in range(size):
            item = start + j
            slot = slots[item]
            row = row_ref[slot] % SHARD
            left = col_ref[slot]
            base = pl.multiple_of((row // 8) * 8, 8)
            weight = (item < count).astype(jnp.float32)
            where.append((slot, base, row % 8, left, weight))

        left_k, right_k = prop_ref[0], prop_ref[1]
        left_d, right_d = dft_ref[0], dft_ref[1]
        wide = None
        for layer in range(SLICES):
            res, ims = [], []
            for j in range(size):
                _, base, rem, left, _ = where[j]
                o_re = cut(0, layer, base, rem, left)
                o_im = cut(1, layer, base, rem, left)
                if layer > 0:
                    piece_save[0, layer - 1, j] = o_re
                    piece_save[1, layer - 1, j] = o_im
                if layer == 0:
                    w_re, w_im = probe_ref[0], probe_ref[1]
                else:
                    w_re = wide[j * PATCH : (j + 1) * PATCH, :PATCH]
                    w_im = wide[j * PATCH : (j + 1) * PATCH, PATCH:]
                res.append(half(w_re * o_re - w_im * o_im))
                ims.append(half(w_re * o_im + w_im * o_re))
            tall = jnp.concatenate(
                [jnp.concatenate(res, axis=1), jnp.concatenate(ims, axis=1)], axis=0
            )
            last = layer + 1 == SLICES
            inner = half(dot(left_d if last else left_k, tall))
            wide = dot(rows_to_lanes(inner, size), right_d if last else right_k)
            if not last:
                wave_save[layer, : size * PATCH] = wide

        parts = []
        for j in range(size):
            slot, _, _, _, weight = where[j]
            far_re = wide[j * PATCH : (j + 1) * PATCH, :PATCH]
            far_im = wide[j * PATCH : (j + 1) * PATCH, PATCH:]
            square = far_re * far_re + far_im * far_im + AMP_FLOOR
            target = measured[slot].astype(jnp.float32)
            scale = weight * (1.0 - target * lax.rsqrt(square))
            parts.append(jnp.concatenate([half(far_re * scale), half(far_im * scale)], axis=1))
        back = jnp.concatenate(parts, axis=0)
        for layer in range(SLICES - 1, -1, -1):
            last = layer + 1 == SLICES
            outer = half(dot(back, left_d if last else left_k))
            cot = dot(right_d if last else right_k, lanes_to_rows(outer, size))
            parts = []
            for j in range(size):
                _, base, rem, left, _ = where[j]
                g_re = cot[:PATCH, j * PATCH : (j + 1) * PATCH]
                g_im = cot[PATCH:, j * PATCH : (j + 1) * PATCH]
                if layer == 0:
                    w_re, w_im = probe_ref[0], probe_ref[1]
                else:
                    w_re = wave_save[layer - 1, j * PATCH : (j + 1) * PATCH, :PATCH]
                    w_im = wave_save[layer - 1, j * PATCH : (j + 1) * PATCH, PATCH:]
                add_back(0, layer, base, rem, left, g_re * w_re + g_im * w_im)
                add_back(1, layer, base, rem, left, g_im * w_re - g_re * w_im)
                if layer > 0:
                    o_re = piece_save[0, layer - 1, j]
                    o_im = piece_save[1, layer - 1, j]
                    parts.append(
                        jnp.concatenate(
                            [half(g_re * o_re + g_im * o_im), half(g_im * o_re - g_re * o_im)],
                            axis=1,
                        )
                    )
            if layer > 0:
                back = jnp.concatenate(parts, axis=0)

    def full_step(step, carry):
        group(step * GROUP, GROUP)
        return carry

    rest = count % GROUP
    steps_full = count // GROUP + (rest > TAIL).astype(jnp.int32)
    lax.fori_loop(0, steps_full, full_step, jnp.int32(0))

    @pl.when(jnp.logical_and(rest > 0, rest <= TAIL))
    def _():
        group(steps_full * GROUP, TAIL)

    store_a = pltpu.make_async_copy(window(total, 0), send_up_hbm, out_sem.at[0])
    store_b = pltpu.make_async_copy(window(total, 2), send_down_hbm, out_sem.at[1])
    store_c = pltpu.make_async_copy(window(total, 1), middle_hbm, out_sem.at[2])
    store_a.start()
    store_b.start()
    store_c.start()
    store_a.wait()
    store_b.wait()
    store_c.wait()


def band_gradient(rows, cols, place, probe, tables, measured, own, across, below, above):
    smem = pl.BlockSpec(memory_space=pltpu.SMEM)
    vmem = pl.BlockSpec(memory_space=pltpu.VMEM)
    hbm = pl.BlockSpec(memory_space=pltpu.HBM)
    part = jax.ShapeDtypeStruct((2, SLICES, SHARD, 2 * PATCH), jnp.float32)
    whole = (2, SLICES, WINDOW, 2 * PATCH)
    return pl.pallas_call(
        body,
        out_shape=(part, part, part),
        in_specs=[smem, smem, smem, vmem, vmem, vmem, hbm, hbm, hbm, hbm, hbm],
        out_specs=(hbm, hbm, hbm),
        scratch_shapes=[
            pltpu.VMEM(whole, jnp.float32),
            pltpu.VMEM(whole, jnp.float32),
            pltpu.VMEM((CAP, PATCH, PATCH), jnp.bfloat16),
            pltpu.VMEM((SLICES - 1, GROUP * PATCH, 2 * PATCH), jnp.float32),
            pltpu.VMEM((2, SLICES - 1, GROUP, PATCH, PATCH), jnp.float32),
            pltpu.SMEM((CAP + GROUP,), jnp.int32),
            pltpu.SemaphoreType.DMA((3,)),
            pltpu.SemaphoreType.DMA((3,)),
            pltpu.SemaphoreType.DMA,
        ],
        compiler_params=pltpu.CompilerParams(vmem_limit_bytes=48 * 1024 * 1024),
        cost_estimate=pl.CostEstimate(
            flops=5_000_000_000, bytes_accessed=8_000_000, transcendentals=0
        ),
    )(rows, cols, place, probe, *tables, measured, own, across, below, above)


def route_pairs(tiles):
    up, down, tile = [], [], []
    for t in range(tiles):
        at = 4 * t
        up += [(at, at + 1), (at + 1, at + 2), (at + 2, at + 3), (at + 3, at)]
        down += [(at + 2, at + 1), (at + 3, at + 2)]
        if t > 0:
            down += [(at, at - 1), (at + 1, at - 4)]
            tile.append((at, at - 4))
    return up, down, tile


def flipped(pairs):
    return [(b, a) for a, b in pairs]


def local(obj_real, obj_imag, probe, fresnel_phase, row_offset, col_offset, live_count, measured):
    up, down, tile = route_pairs(lax.axis_size("tile"))
    own = jnp.stack([obj_real, obj_imag])
    below = lax.ppermute(own, AXES, down)
    across = lax.ppermute(own, AXES, tile)
    above = lax.ppermute(own, AXES, up)
    member = lax.axis_index("pos").astype(jnp.int32)
    place = jnp.stack([member, live_count[0]])
    tables = stacked_tables(fresnel_phase)
    send_up, send_down, middle = band_gradient(
        row_offset, col_offset, place, probe, tables, measured, own, across, below, above
    )
    back_down = lax.ppermute(send_down, AXES, flipped(down))
    back_tile = lax.ppermute(middle, AXES, flipped(tile))
    back_up = lax.ppermute(send_up, AXES, flipped(up))
    back_up, back_tile, back_down = lax.optimization_barrier(
        (back_up, back_tile, back_down)
    )

    def sum_of(part):
        mid = jnp.where(member == 0, back_tile[part], middle[part])
        return mid + back_down[part] + back_up[part]

    return sum_of(0), sum_of(1)


def solution(mesh):
    rows = P(None, AXES, None)
    in_specs = (rows, rows, P(), P(), P("tile"), P("tile"), P("tile"), P("tile", None, None))
    return jax.shard_map(
        local, mesh=mesh, in_specs=in_specs, out_specs=(rows, rows), check_vma=False
    )
```
